256 devices in a mesh: seq: 32 (over z, y), dp: 8 (over x, core).
Axes of the slice: x: 4, y: 4, z: 8, core: 2. Of those that a mesh axis runs over, the one named last changes fastest.
Arguments:
- q_in: bfloat16 [8, 12288, 1536], P('dp', 'seq')
- k_in: bfloat16 [8, 12288, 1536], P('dp', 'seq')
- v_in: bfloat16 [8, 12288, 1536], P('dp', 'seq'), may hold values from -6 to 6
- q_gain: float32 [128], replicated, may hold values from 0.4 to 5
- k_gain: float32 [128], replicated, may hold values from 0.4 to 5
- window: int32 [8, 32, 3], P('dp', 'seq'), may hold values from -1 to 30, as said below
- grad_out: bfloat16 [8, 12288, 1536], P('dp', 'seq'), may hold values from -6 to 6
Outputs:
- attn_out: bfloat16 [8, 12288, 1536], P('dp', 'seq')
- grad_q: bfloat16 [8, 12288, 1536], P('dp', 'seq')
- grad_k: bfloat16 [8, 12288, 1536], P('dp', 'seq')
- grad_v: bfloat16 [8, 12288, 1536], P('dp', 'seq')
- grad_q_gain: float32 [128], replicated
- grad_k_gain: float32 [128], replicated
The draws below stay inside these ranges and needn't reach their ends.
Inputs may be any that keep to these rules, and one draw needn't show every extreme that they name: `window`: entry j of tile t's list is -1 or t - 1 (j = 0), t - 2 (j = 1), t - 2 * 2 (j = 2); it is -1 where that tile lies outside the grid, and some present neighbours are left out.
All inputs are finite; a program needn't handle non-finite values.
Results may differ from the reference program's by a relative error of at most 0.0054.
The reference program's roundings to bfloat16 on the way (of `probs_low` and `grad_scores`) count: a program that leaves them out, or rounds other values in their place, can miss the bound.
Values may be sent and summed in bfloat16 or wider, within the bound.
No kernel may reach another device: no remote copies, remote signals or barrier semaphores. Data moves between devices by JAX's collectives and lax.ppermute only.
A program may use at most 128 MiB of HBM per device.

```python
import jax
import jax.numpy as jnp
from jax import lax

HEADS = 12
HEAD_DIM = 128
HD = 1536
TILE_TOK = 384
GRID_W = 2
GRID_H = 2
TILES = 32
TOKENS = 12288
BATCH = 8


def shared_keys(key):
    shape_five = (BATCH, TILES, TILE_TOK, HEADS, HEAD_DIM)
    noise = jax.random.normal(jax.random.fold_in(key, 21), shape_five, jnp.float32)
    row_scale = jnp.exp(jax.random.uniform(jax.random.fold_in(key, 22), (BATCH, TILES, TILE_TOK, HEADS, 1), jnp.float32, -1.2, 1.2))
    keys_raw = noise * row_scale
    return keys_raw


def draw_k_in(key, part):
    keys_raw = shared_keys(key)
    return jnp.clip(keys_raw, -16.0, 16.0).reshape(BATCH, TOKENS, HD).astype(jnp.bfloat16)


def draw_q_in(key, part):
    shape_five = (BATCH, TILES, TILE_TOK, HEADS, HEAD_DIM)
    noise = jax.random.normal(jax.random.fold_in(key, 24), shape_five, jnp.float32)
    row_scale = jnp.exp(jax.random.uniform(jax.random.fold_in(key, 25), (BATCH, TILES, TILE_TOK, HEADS, 1), jnp.float32, -1.2, 1.2))
    queries = noise * row_scale
    return jnp.clip(queries, -16.0, 16.0).reshape(BATCH, TOKENS, HD).astype(jnp.bfloat16)


def gain_draw(key, salt):
    low_end, high_end = (0.4, 2.0)
    spread = jax.random.uniform(jax.random.fold_in(key, salt), (HEAD_DIM,), jnp.float32, jnp.log(low_end), jnp.log(high_end))
    return jnp.clip(jnp.exp(spread), 0.4, 5.0)


def draw_q_gain(key, part):
    return gain_draw(key, 11)


def draw_k_gain(key, part):
    return gain_draw(key, 12)


def draw_window(key, part):
    tile_ids = jnp.arange(TILES, dtype=jnp.int32)
    lead = GRID_W * GRID_H
    geometry = jnp.stack([tile_ids % GRID_W > 0, tile_ids // GRID_W % GRID_H > 0, tile_ids // lead > 0], axis=-1)
    steps_back = jnp.array([1, GRID_W, lead], jnp.int32)
    keep = jax.random.randint(jax.random.fold_in(key, 31), (BATCH, TILES, 3), 0, 4) > 0
    keep = keep | (tile_ids == TILES - 1)[None, :, None]
    entries = jnp.where(geometry[None] & keep, tile_ids[None, :, None] - steps_back[None, None, :], -1)
    return entries.astype(jnp.int32)


def shard_levels(own_key, dims, cuts, low, top_value):
    factor_of, own = 1.0, jax.random.fold_in(own_key, 6)
    for position, shards_of in cuts:
        heights = jnp.exp(jax.random.uniform(jax.random.fold_in(own, position), (shards_of,), jnp.float32, low / len(cuts), top_value / len(cuts)))
        factor_of = factor_of * jnp.repeat(heights, dims[position] // shards_of).reshape([-1 if axis == position else 1 for axis in range(len(dims))])
    return factor_of


def scatter_about(rng, dims, scale, limit, cuts=(), kind=jnp.bfloat16):
    values = scale * jax.random.normal(rng, dims, jnp.float32)
    if cuts:
        values = values * shard_levels(rng, dims, cuts, -0.22, 0.18)
    return jnp.clip(values, -limit, limit).astype(kind)


def setup_inputs(seed: int = 0) -> dict:
    splits = jax.random.split(jax.random.key(seed), 8)
    q_in = draw_q_in(jax.random.fold_in(splits[7], 71), 0)
    k_in = draw_k_in(jax.random.fold_in(splits[7], 71), 0)
    v_in = scatter_about(splits[2], (BATCH, TOKENS, HD), 1.0, 6.0, ((0, 8), (1, 32)))
    q_gain = draw_q_gain(jax.random.fold_in(splits[7], 71), 0)
    k_gain = draw_k_gain(jax.random.fold_in(splits[7], 71), 0)
    window = draw_window(jax.random.fold_in(splits[7], 71), 0)
    grad_out = scatter_about(splits[6], (BATCH, TOKENS, HD), 1.0, 6.0, ((0, 8), (1, 32)))
    return dict(q_in=q_in, k_in=k_in, v_in=v_in, q_gain=q_gain, k_gain=k_gain, window=window, grad_out=grad_out)


def normalize(rows, gain_vec):
    flat = rows.astype(jnp.float32).reshape(rows.shape[:-1] + (-1, HEAD_DIM))
    root = lax.rsqrt(lax.optimization_barrier(jnp.mean(flat * flat, axis=-1, keepdims=True)) + 1e-06)
    unit = flat * root
    return (unit * gain_vec, unit, root)

def norm_backward(grad_norm, unit, root, gain_vec):
    scaled = grad_norm * gain_vec
    inner = lax.optimization_barrier(jnp.mean(scaled * unit, axis=-1, keepdims=True))
    return (root * (scaled - unit * inner), lax.optimization_barrier(jnp.sum(grad_norm * unit, axis=(0, 1))))

def reference(q_in, k_in, v_in, q_gain, k_gain, window, grad_out):
    score_scale = HEAD_DIM ** (-0.5)
    lead = GRID_W * GRID_H
    offsets = (1, GRID_W, lead)

    def one_sample(pieces):
        q_rows, k_rows, v_rows, lists, g_rows = pieces
        q_norm, q_unit, q_root = normalize(q_rows, q_gain)
        k_norm, k_unit, k_root = normalize(k_rows, k_gain)
        q_tiles = q_norm.astype(jnp.bfloat16).reshape(TILES, TILE_TOK, HD)
        k_tiles = k_norm.astype(jnp.bfloat16).reshape(TILES, TILE_TOK, HD)
        v_tiles = v_rows.reshape(TILES, TILE_TOK, HD)
        g_tiles = g_rows.reshape(TILES, TILE_TOK, HD)
        zero_tiles = jnp.zeros((lead, TILE_TOK, HD), jnp.bfloat16)
        k_padded = jnp.concatenate([zero_tiles, k_tiles], axis=0)
        v_padded = jnp.concatenate([zero_tiles, v_tiles], axis=0)

        def one_tile(index):
            keys = jnp.stack([k_tiles[index]] + [k_padded[index + lead - step] for step in offsets])
            vals = jnp.stack([v_tiles[index]] + [v_padded[index + lead - step] for step in offsets])
            key_valid = jnp.concatenate([jnp.ones((1,), bool), lists[index] >= 0])
            key_mask = jnp.broadcast_to(key_valid[:, None], (4, TILE_TOK)).reshape(4 * TILE_TOK)
            q_head = q_tiles[index].astype(jnp.float32).reshape(TILE_TOK, HEADS, HEAD_DIM)
            k_head = keys.astype(jnp.float32).reshape(4 * TILE_TOK, HEADS, HEAD_DIM)
            v_head = vals.astype(jnp.float32).reshape(4 * TILE_TOK, HEADS, HEAD_DIM)
            g_head = g_tiles[index].astype(jnp.float32).reshape(TILE_TOK, HEADS, HEAD_DIM)
            scores = jnp.einsum('qhd,khd->hqk', q_head, k_head) * score_scale
            scores = jnp.where(key_mask[None, None, :], scores, -jnp.inf)
            row_max = lax.optimization_barrier(jnp.max(scores, axis=-1, keepdims=True))
            weights_raw = jnp.exp(scores - row_max)
            probs = weights_raw / lax.optimization_barrier(jnp.sum(weights_raw, axis=-1, keepdims=True))
            probs_low = lax.optimization_barrier(probs.astype(jnp.bfloat16)).astype(jnp.float32)
            out_low = jnp.einsum('hqk,khd->qhd', probs_low, v_head).astype(jnp.bfloat16)
            row_dot = jnp.einsum('qhd,qhd->hq', g_head, out_low.astype(jnp.float32))
            grad_probs = jnp.einsum('qhd,khd->hqk', g_head, v_head)
            grad_scores = probs * (grad_probs - row_dot[..., None]) * score_scale
            grad_scores = lax.optimization_barrier(grad_scores.astype(jnp.bfloat16)).astype(jnp.float32)
            grad_qhead = jnp.einsum('hqk,khd->qhd', grad_scores, k_head)
            key_terms = jnp.einsum('hqk,qhd->khd', grad_scores, q_head).astype(jnp.bfloat16).reshape(4, TILE_TOK, HD)
            val_terms = jnp.einsum('hqk,qhd->khd', probs_low, g_head).astype(jnp.bfloat16).reshape(4, TILE_TOK, HD)
            return (out_low.reshape(TILE_TOK, HD), grad_qhead, key_terms, val_terms)
        attn_tiles, grad_qheads, key_terms, val_terms = lax.map(one_tile, jnp.arange(TILES))
        key_sum = key_terms[:, 0].astype(jnp.float32)
        val_sum = val_terms[:, 0].astype(jnp.float32)
        for direction, step in enumerate(offsets):
            zero_rows = jnp.zeros((step, TILE_TOK, HD), jnp.float32)
            key_sum = key_sum + jnp.concatenate([key_terms[step:, direction + 1].astype(jnp.float32), zero_rows], axis=0)
            val_sum = val_sum + jnp.concatenate([val_terms[step:, direction + 1].astype(jnp.float32), zero_rows], axis=0)
        grad_qnorm = grad_qheads.reshape(TOKENS, HEADS, HEAD_DIM)
        grad_knorm = key_sum.reshape(TOKENS, HEADS, HEAD_DIM)
        q_back, q_gain_part = norm_backward(grad_qnorm, q_unit, q_root, q_gain)
        k_back, k_gain_part = norm_backward(grad_knorm, k_unit, k_root, k_gain)
        return (attn_tiles.reshape(TOKENS, HD), q_back.reshape(TOKENS, HD).astype(jnp.bfloat16), k_back.reshape(TOKENS, HD).astype(jnp.bfloat16), val_sum.reshape(TOKENS, HD).astype(jnp.bfloat16), q_gain_part, k_gain_part)
    results = lax.map(one_sample, (q_in, k_in, v_in, window, grad_out))
    return (results[0], results[1], results[2], results[3], lax.optimization_barrier(jnp.sum(results[4], axis=0)), lax.optimization_barrier(jnp.sum(results[5], axis=0)))
```

```python
import functools
import math

import jax
import jax.numpy as jnp
from jax import lax
from jax.experimental import pallas as pl
from jax.experimental.pallas import tpu as pltpu
from jax.sharding import PartitionSpec as P

HEAD_DIM = 128
ROW = 4
SPLITS = (4, 4, 4)
F32 = jnp.float32
BF16 = jnp.bfloat16

KEYS_OUT = ((0, 1), (1, 0), (2, 3))
KEYS_ON = ((1, 2), (0, 3))
TERMS_OUT = ((3, 0), (2, 1))
TERMS_ON = ((0, 1), (1, 0), (3, 2))


def dot(a, b):
    return lax.dot_general(a, b, (((1,), (0,)), ((), ())), preferred_element_type=F32)


def unit_rows(block):
    flat = block.astype(F32)
    root = lax.rsqrt(jnp.mean(flat * flat, axis=1, keepdims=True) + 1e-6)
    return flat * root, root


def attn_kernel(win, q_ref, k_ref, v_ref, g_ref, kv1, kv2, kv4, qg_ref, kg_ref, *refs):
    refs = refs[2:] if len(refs) == 17 else refs
    (out_ref, gq_ref, own_ref, t1_ref, t2_ref, t4_ref, qsum_ref, ksum_ref) = refs[:8]
    (s_ref, p_ref, kb_ref, kt_ref, m_ref, l_ref, acc_ref) = refs[8:]
    step = pl.program_id(0)
    scale = HEAD_DIM ** (-0.5)
    to_two = scale * math.log2(math.e)

    @pl.when(step == 0)
    def _():
        qsum_ref[...] = jnp.zeros_like(qsum_ref)
        ksum_ref[...] = jnp.zeros_like(ksum_ref)

    q_gain = qg_ref[...]
    k_gain = kg_ref[...]
    qt = q_ref[...].T.astype(F32)
    q_root = lax.rsqrt(jnp.mean(qt * qt, axis=0, keepdims=True) + 1e-6)
    q_unit = qt * q_root
    qt_b = (q_unit * q_gain).astype(BF16)
    q_b = qt_b.T
    g_b = g_ref[...]
    gt_b = g_b.T

    def keys(j):
        return k_ref[...] if j == 0 else (kv1, kv2, kv4)[j - 1][0]

    def vals(j):
        return v_ref[...] if j == 0 else (kv1, kv2, kv4)[j - 1][1]

    terms = (own_ref, t1_ref, t2_ref, t4_ref)

    def each(body, otherwise=None):
        body(0)
        for j in range(1, 4):
            pl.when(win[j - 1] >= 0)(functools.partial(body, j))
            if otherwise is not None:
                pl.when(win[j - 1] < 0)(functools.partial(otherwise, j))

    def scores(j):
        unit, _ = unit_rows(keys(j))
        k_b = (unit * k_gain).astype(BF16)
        kb_ref[j] = k_b
        kt_ref[j] = k_b.T
        s = dot(k_b, qt_b)
        s_ref[j] = s
        top = jnp.max(s, axis=0, keepdims=True)
        m_ref[...] = top if j == 0 else jnp.maximum(m_ref[...], top)

    each(scores)
    m_ref[...] = m_ref[...] * to_two

    def powers(j):
        e = jnp.exp2(s_ref[j] * to_two - m_ref[...])
        s_ref[j] = e
        total = jnp.sum(e, axis=0, keepdims=True)
        l_ref[...] = total if j == 0 else l_ref[...] + total

    each(powers)
    l_ref[...] = 1.0 / l_ref[...]

    def forward(j):
        p = (s_ref[j] * l_ref[...]).astype(BF16)
        p_ref[j] = p
        o = dot(vals(j).T, p)
        acc_ref[...] = o if j == 0 else acc_ref[...] + o

    each(forward)
    out_low = acc_ref[...].astype(BF16)
    out_ref[...] = out_low.T
    row_dot = jnp.sum(gt_b.astype(F32) * out_low.astype(F32), axis=0, keepdims=True)
    m_ref[...] = row_dot

    def backward(j):
        dp = dot(vals(j), gt_b)
        ds = ((s_ref[j] * l_ref[...]) * (dp - m_ref[...]) * scale).astype(BF16)
        dq = dot(kt_ref[j], ds)
        acc_ref[...] = dq if j == 0 else acc_ref[...] + dq
        dk = dot(ds, q_b).astype(BF16)
        terms[j][0] = dk
        terms[j][1] = dot(p_ref[j], g_b).astype(BF16)
        unit, _ = unit_rows(keys(j))
        ksum_ref[...] += jnp.sum((dk.astype(F32) * unit).reshape(-1, 8, HEAD_DIM), axis=0)

    def nothing(j):
        terms[j][...] = jnp.zeros_like(terms[j])

    each(backward, nothing)
    dq = acc_ref[...]
    qsum_ref[...] += dq * q_unit
    scaled = dq * q_gain
    inner = jnp.mean(scaled * q_unit, axis=0, keepdims=True)
    gq_ref[...] = (q_root * (scaled - q_unit * inner)).astype(BF16).T


def attn_part(first, heads, win, q, k, v, g, pairs, q_gain, k_gain, filled):
    rows, width = q.shape
    part = heads * HEAD_DIM
    whole = pl.BlockSpec((rows, HEAD_DIM), lambda h: (0, first + h))
    two = pl.BlockSpec((2, rows, HEAD_DIM), lambda h: (0, 0, h))
    smem = pl.BlockSpec(memory_space=pltpu.SMEM)
    hbm = pl.BlockSpec(memory_space=pl.ANY)

    def const(shape):
        return pl.BlockSpec(shape, lambda h: (0, 0))

    full = jax.ShapeDtypeStruct((rows, width), BF16)
    pair = jax.ShapeDtypeStruct((2, rows, part), BF16)
    filled = () if filled is None else filled
    return pl.pallas_call(
        attn_kernel,
        grid=(heads,),
        in_specs=[smem, whole, whole, whole, whole, two, two, two, const((HEAD_DIM, 1)), const((1, HEAD_DIM))]
        + [hbm] * len(filled),
        out_specs=[whole, whole, two, two, two, two, const((HEAD_DIM, rows)), const((8, HEAD_DIM))],
        out_shape=[
            full,
            full,
            pair,
            pair,
            pair,
            pair,
            jax.ShapeDtypeStruct((HEAD_DIM, rows), F32),
            jax.ShapeDtypeStruct((8, HEAD_DIM), F32),
        ],
        scratch_shapes=[
            pltpu.VMEM((4, rows, rows), F32),
            pltpu.VMEM((4, rows, rows), BF16),
            pltpu.VMEM((4, rows, HEAD_DIM), BF16),
            pltpu.VMEM((4, HEAD_DIM, rows), BF16),
            pltpu.VMEM((1, rows), F32),
            pltpu.VMEM((1, rows), F32),
            pltpu.VMEM((HEAD_DIM, rows), F32),
        ],
        input_output_aliases={10 + i: i for i in range(len(filled))},
        compiler_params=pltpu.CompilerParams(
            dimension_semantics=("arbitrary",), vmem_limit_bytes=24 * 2**20
        ),
        cost_estimate=pl.CostEstimate(
            flops=heads * 12 * 4 * rows * rows * HEAD_DIM * 3,
            bytes_accessed=heads * rows * HEAD_DIM * 2 * 20,
            transcendentals=heads * 4 * rows * rows,
        ),
        name="attention_part",
    )(win, q, k, v, g, *pairs, q_gain.reshape(HEAD_DIM, 1), k_gain.reshape(1, HEAD_DIM), *filled)


def close_kernel(k_ref, own, got_y, got_z, kg_ref, *refs):
    gk_ref, gv_ref = refs[-2:]
    dk = own[0].astype(F32) + got_y[0].astype(F32) + got_z[0].astype(F32)
    dv = own[1].astype(F32) + got_y[1].astype(F32) + got_z[1].astype(F32)
    gv_ref[...] = dv.astype(BF16)
    unit, root = unit_rows(k_ref[...])
    scaled = dk * kg_ref[...]
    inner = jnp.mean(scaled * unit, axis=1, keepdims=True)
    gk_ref[...] = (root * (scaled - unit * inner)).astype(BF16)


def close_part(first, heads, k, own, got_y, got_z, k_gain, filled):
    rows, width = k.shape
    whole = pl.BlockSpec((rows, HEAD_DIM), lambda h: (0, first + h))
    two = pl.BlockSpec((2, rows, HEAD_DIM), lambda h: (0, 0, h))
    hbm = pl.BlockSpec(memory_space=pl.ANY)
    full = jax.ShapeDtypeStruct((rows, width), BF16)
    filled = () if filled is None else filled
    return pl.pallas_call(
        close_kernel,
        grid=(heads,),
        in_specs=[whole, two, two, two, pl.BlockSpec((1, HEAD_DIM), lambda h: (0, 0))] + [hbm] * len(filled),
        out_specs=[whole, whole],
        out_shape=[full, full],
        input_output_aliases={5 + i: i for i in range(len(filled))},
        compiler_params=pltpu.CompilerParams(dimension_semantics=("arbitrary",), vmem_limit_bytes=16 * 2**20),
        cost_estimate=pl.CostEstimate(
            flops=heads * rows * HEAD_DIM * 20,
            bytes_accessed=heads * rows * HEAD_DIM * 2 * 9,
            transcendentals=heads * rows,
        ),
        name="close_part",
    )(k, own, got_y, got_z, k_gain.reshape(1, HEAD_DIM), *filled)


def on_device(q_in, k_in, v_in, q_gain, k_gain, window, grad_out):
    q, k, v, g = q_in[0], k_in[0], v_in[0], grad_out[0]
    win = window[0, 0]
    tiles = lax.axis_size("seq")
    starts = range(0, tiles, ROW)

    def in_row(block, hops):
        return lax.ppermute(block, "seq", [(s + a, s + b) for s in starts for a, b in hops])

    def frames(block, step):
        return lax.ppermute(
            block, "seq", [(t, t + step) for t in range(tiles) if 0 <= t + step < tiles]
        )

    firsts = [sum(SPLITS[:i]) for i in range(len(SPLITS))]
    fetched = []
    for first, heads in zip(firsts, SPLITS):
        cols = slice(first * HEAD_DIM, (first + heads) * HEAD_DIM)
        mine = jnp.stack([k[:, cols], v[:, cols]])
        near = in_row(mine, KEYS_OUT)
        back = frames(mine, ROW)
        far = in_row(near, KEYS_ON)
        fetched.append((near, far, back))
    filled, sums, held = None, [], []
    for first, heads, pairs in zip(firsts, SPLITS, fetched):
        out = attn_part(first, heads, win, q, k, v, g, pairs, q_gain, k_gain, filled)
        filled = tuple(out[:2])
        own, near, far, back = out[2:6]
        sums.append((jnp.sum(out[6], axis=1), jnp.sum(out[7], axis=0)))
        via = in_row(far, TERMS_OUT)
        got_z = frames(back, -ROW)
        onward = (near.astype(F32) + via.astype(F32)).astype(BF16)
        got_y = in_row(onward, TERMS_ON)
        held.append((own, got_y, got_z))
    gains = jnp.stack([sum(s[0] for s in sums), sum(s[1] for s in sums)])
    gains = lax.psum(gains, ("seq", "dp"))
    closed = None
    for first, heads, got in zip(firsts, SPLITS, held):
        closed = tuple(close_part(first, heads, k, *got, k_gain, closed))
    return (filled[0][None], filled[1][None], closed[0][None], closed[1][None], gains[0], gains[1])


def solution(mesh):
    rows = P("dp", "seq", None)
    return jax.shard_map(
        on_device,
        mesh=mesh,
        in_specs=(rows, rows, rows, P(), P(), rows, rows),
        out_specs=(rows, rows, rows, rows, P(), P()),
        check_vma=False,
    )
```

```python
import functools
import math

import jax
import jax.numpy as jnp
from jax import lax
from jax.experimental import pallas as pl
from jax.experimental.pallas import tpu as pltpu
from jax.sharding import PartitionSpec as P

HEAD_DIM = 128
ROW = 4
SPLITS = (4, 4, 4)
Z_KEYS = ((0,), (1, 2))
Z_TERMS = ((0, 1), (2,))
RELAY_KEYS = (True, True, True)
RELAY_TERMS = (True, True, False)
ORDERED = True
CLOSE_BEFORE = {}
CLOSE_AFTER = (0, 1)
CLOSE_LAST = (2,)
RADIX = {"dp": 2, "seq": 4}
TAIL = ((0, ("on",)), (3, ("y", "z", "c")))
ATTN_COST = 4_000_000_000
CLOSE_COST = 1_000_000_000
F32 = jnp.float32
BF16 = jnp.bfloat16
MIB = 2**20

KEYS_OUT = ((0, 1), (1, 0), (2, 3))
KEYS_ON = ((1, 2), (0, 3))
TERMS_OUT = ((3, 0), (2, 1))
TERMS_ON = ((0, 1), (1, 0), (3, 2))
STEP_ONE = ((0, 1), (2, 3))
STEP_TWO = ((0, 2), (1, 3))


def dot(a, b):
    return lax.dot_general(a, b, (((1,), (0,)), ((), ())), preferred_element_type=F32)


def unit_rows(block):
    flat = block.astype(F32)
    root = lax.rsqrt(jnp.mean(flat * flat, axis=1, keepdims=True) + 1e-6)
    return flat * root, root


def attn_kernel(per_step, begun, win, q_ref, k_ref, v_ref, g_ref, kv1, kv2, kv4, qg_ref, kg_ref, *refs):
    (out_ref, gq_ref, own_ref, t1_ref, t2_ref, t4_ref, qsum_ref, ksum_ref) = refs[-8:]
    scale = HEAD_DIM ** (-0.5)
    to_two = scale * math.log2(math.e)

    @pl.when(pl.program_id(0) == 0)
    def _():
        qsum_ref[...] = refs[0][...] if begun else jnp.zeros_like(qsum_ref)
        ksum_ref[...] = refs[1][...] if begun else jnp.zeros_like(ksum_ref)

    q_gain = qg_ref[...]
    k_gain = kg_ref[...]
    held = [True] + [win[j] >= 0 for j in range(3)]
    terms = (own_ref, t1_ref, t2_ref, t4_ref)
    for at in range(per_step):
        cols = slice(at * HEAD_DIM, (at + 1) * HEAD_DIM)
        qt = q_ref[:, cols].T.astype(F32)
        q_root = lax.rsqrt(jnp.mean(qt * qt, axis=0, keepdims=True) + 1e-6)
        q_unit = qt * q_root
        qt_b = (q_unit * q_gain).astype(BF16)
        q_b = qt_b.T
        g_b = g_ref[:, cols]
        gt_b = g_b.T
        keys = [k_ref[:, cols]] + [ref[0, :, cols] for ref in (kv1, kv2, kv4)]
        vals = [v_ref[:, cols]] + [ref[1, :, cols] for ref in (kv1, kv2, kv4)]

        k_norm, scores, tops = [], [], []
        for j in range(4):
            k_norm.append((unit_rows(keys[j])[0] * k_gain).astype(BF16))
            scores.append(dot(k_norm[j], qt_b))
            top = jnp.max(scores[j], axis=0, keepdims=True)
            tops.append(top if j == 0 else jnp.where(held[j], top, -jnp.inf))
        row_max = functools.reduce(jnp.maximum, tops) * to_two
        raw, sums, dps = [], [], []
        for j in range(4):
            dps.append(dot(vals[j], gt_b))
            factor = to_two if j == 0 else jnp.where(held[j], to_two, 0.0)
            less = row_max if j == 0 else jnp.where(held[j], row_max, 1e30)
            raw.append(jnp.exp2(scores[j] * factor - less))
            sums.append(jnp.sum(raw[j], axis=0, keepdims=True))
        inverse = 1.0 / functools.reduce(jnp.add, sums)
        out = None
        for j in range(4):
            probs_low = (raw[j] * inverse).astype(BF16)
            terms[j][at, 1] = dot(probs_low, g_b).astype(BF16)
            o = dot(vals[j].T, probs_low)
            out = o if j == 0 else out + o
        out_low = out.astype(BF16)
        out_ref[:, cols] = out_low.T
        row_dot = jnp.sum(gt_b.astype(F32) * out_low.astype(F32), axis=0, keepdims=True)
        scaled_inverse = inverse * scale
        dq = None
        k_part = None
        for j in range(4):
            ds = (raw[j] * ((dps[j] - row_dot) * scaled_inverse)).astype(BF16)
            d = dot(k_norm[j].T, ds)
            dq = d if j == 0 else dq + d
            dk = dot(ds, q_b).astype(BF16)
            terms[j][at, 0] = dk
            part = jnp.sum((dk.astype(F32) * unit_rows(keys[j])[0]).reshape(-1, 8, HEAD_DIM), axis=0)
            k_part = part if j == 0 else k_part + part
        ksum_ref[...] += k_part
        qsum_ref[...] += dq * q_unit
        scaled = dq * q_gain
        inner = jnp.mean(scaled * q_unit, axis=0, keepdims=True)
        gq_ref[:, cols] = (q_root * (scaled - q_unit * inner)).astype(BF16).T


def attn_part(first, heads, win, q, k, v, g, pairs, z_at, q_gain, k_gain, filled, t4_shape, t4_at, t4_filled, totals):
    rows, width = q.shape
    per_step = next(n for n in (2, 1) if not any(x % n for x in (first, heads, z_at, t4_at)))
    wide = per_step * HEAD_DIM
    whole = pl.BlockSpec((rows, wide), lambda h: (0, first // per_step + h))
    smem = pl.BlockSpec(memory_space=pltpu.SMEM)
    hbm = pl.BlockSpec(memory_space=pl.ANY)

    def two_at(start):
        return pl.BlockSpec((per_step, 2, rows, HEAD_DIM), lambda h: (start // per_step + h, 0, 0, 0))

    def keys_at(start):
        return pl.BlockSpec((2, rows, wide), lambda h: (0, 0, start // per_step + h))

    def const(shape):
        return pl.BlockSpec(shape, lambda h: (0, 0))

    full = jax.ShapeDtypeStruct((rows, width), BF16)
    pair = jax.ShapeDtypeStruct((heads, 2, rows, HEAD_DIM), BF16)
    sums = [(HEAD_DIM, rows), (8, HEAD_DIM)]
    begun = totals is not None
    more = list(totals) if begun else []
    more_specs = [const(x) for x in sums] if begun else []
    kept = {6: 10, 7: 11} if begun else {}
    for out, array in ((0, filled and filled[0]), (1, filled and filled[1]), (5, t4_filled)):
        if array is not None:
            kept[out] = 10 + len(more)
            more.append(array)
            more_specs.append(hbm)
    return pl.pallas_call(
        functools.partial(attn_kernel, per_step, begun),
        grid=(heads // per_step,),
        in_specs=[smem, whole, whole, whole, whole, keys_at(0), keys_at(0), keys_at(z_at)]
        + [const((HEAD_DIM, 1)), const((1, HEAD_DIM))]
        + more_specs,
        out_specs=[whole, whole, two_at(0), two_at(0), two_at(0), two_at(t4_at)] + [const(x) for x in sums],
        out_shape=[
            full,
            full,
            pair,
            pair,
            pair,
            jax.ShapeDtypeStruct((t4_shape, 2, rows, HEAD_DIM), BF16),
            *[jax.ShapeDtypeStruct(x, F32) for x in sums],
        ],
        input_output_aliases={where: out for out, where in kept.items()},
        compiler_params=pltpu.CompilerParams(
            dimension_semantics=("arbitrary",), vmem_limit_bytes=58 * MIB
        ),
        cost_estimate=pl.CostEstimate(
            flops=heads * ATTN_COST,
            bytes_accessed=heads * ATTN_COST // 1000,
            transcendentals=0,
        ),
        name="attention_part",
    )(win, q, k, v, g, *pairs, q_gain.reshape(HEAD_DIM, 1), k_gain.reshape(1, HEAD_DIM), *more)


def close_kernel(count, k_ref, *refs):
    got, kg_ref, (gk_ref, gv_ref) = refs[:count], refs[count], refs[-2:]
    dk, dv = (functools.reduce(jnp.add, [r[0, i].astype(F32) for r in got]) for i in range(2))
    gv_ref[...] = dv.astype(BF16)
    unit, root = unit_rows(k_ref[...])
    scaled = dk * kg_ref[...]
    inner = jnp.mean(scaled * unit, axis=1, keepdims=True)
    gk_ref[...] = (root * (scaled - unit * inner)).astype(BF16)


def close_part(first, heads, k, got, z_at, k_gain, filled):
    rows, width = k.shape
    whole = pl.BlockSpec((rows, HEAD_DIM), lambda h: (0, first + h))
    two = pl.BlockSpec((1, 2, rows, HEAD_DIM), lambda h: (h, 0, 0, 0))
    two_z = pl.BlockSpec((1, 2, rows, HEAD_DIM), lambda h: (z_at + h, 0, 0, 0))
    hbm = pl.BlockSpec(memory_space=pl.ANY)
    full = jax.ShapeDtypeStruct((rows, width), BF16)
    filled = () if filled is None else filled
    count = len(got)
    return pl.pallas_call(
        functools.partial(close_kernel, count),
        grid=(heads,),
        in_specs=[whole] + [two] * (count - 1) + [two_z] + [pl.BlockSpec((1, HEAD_DIM), lambda h: (0, 0))] + [hbm] * len(filled),
        out_specs=[whole, whole],
        out_shape=[full, full],
        input_output_aliases={2 + count + i: i for i in range(len(filled))},
        compiler_params=pltpu.CompilerParams(dimension_semantics=("arbitrary",), vmem_limit_bytes=58 * MIB),
        cost_estimate=pl.CostEstimate(
            flops=heads * CLOSE_COST,
            bytes_accessed=heads * CLOSE_COST // 1000,
            transcendentals=0,
        ),
        name="close_part",
    )(k, *got, k_gain.reshape(1, HEAD_DIM), *filled)


def total_over_mesh(block, waits):
    def spread(x, axis, size, stride, group):
        def peer(i, d):
            at = i // stride % group
            return i + ((at ^ d) - at) * stride

        got = [x] + [lax.ppermute(x, axis, [(i, peer(i, d)) for i in range(size)]) for d in range(1, group)]
        while len(got) > 1:
            got = [a + b for a, b in zip(got[::2], got[1::2])]
        return got[0]

    def whole_axis(x, axis, size):
        stride = 1
        while stride < size:
            group = 4 if RADIX[axis] == 4 and size // stride % 4 == 0 else 2
            x = spread(after(x, *waits.pop(0)), axis, size, stride, group)
            stride *= group
        return x

    block = whole_axis(block, "dp", lax.axis_size("dp"))
    return whole_axis(block, "seq", lax.axis_size("seq"))


def after(block, *others):
    return lax.optimization_barrier((block,) + others)[0] if ORDERED and others else block


def on_device(q_in, k_in, v_in, q_gain, k_gain, window, grad_out):
    q, k, v, g = q_in[0], k_in[0], v_in[0], grad_out[0]
    rows = q.shape[0]
    win = window[0, 0]
    tiles = lax.axis_size("seq")
    starts = range(0, tiles, ROW)

    def in_row(block, hops):
        return lax.ppermute(block, "seq", [(s + a, s + b) for s in starts for a, b in hops])

    def frames(block, step):
        return lax.ppermute(
            block, "seq", [(t, t + step) for t in range(tiles) if 0 <= t + step < tiles]
        )

    def back_of(hops):
        return tuple((b, a) for a, b in hops)

    firsts = [sum(SPLITS[:i]) for i in range(len(SPLITS))]
    parts = range(len(SPLITS))
    last = len(SPLITS) - 1
    near, far, back, outs, onward, sent, got_z = {}, {}, {}, {}, {}, {}, {}

    def place(groups, i):
        group = next(g for g in groups if i in g)
        sizes = [SPLITS[j] for j in group]
        return group, sum(sizes), sum(sizes[: group.index(i)])

    def pack(first, heads):
        cols = slice(first * HEAD_DIM, (first + heads) * HEAD_DIM)
        return jnp.stack([x[:, cols] for x in (k, v)])

    for i in parts:
        mine = pack(firsts[i], SPLITS[i])
        along = mine if i == 0 else after(mine, near[i - 1])
        group, heads, _ = place(Z_KEYS, i)
        if i == group[0]:
            ours = mine if heads == SPLITS[i] else pack(firsts[i], heads)
            if i > 0:
                ours = after(ours, *list(back.values())[-1:], near[max(group[0] - 1, 0)])
            back[group] = frames(ours, ROW)
        if RELAY_KEYS[i]:
            near[i] = in_row(along, KEYS_OUT)
            far[i] = in_row(near[i], KEYS_ON)
        else:
            near[i] = in_row(along, STEP_ONE)
            far[i] = in_row(along, STEP_TWO)

    vias = {}

    def relay(i, *tokens):
        own, to_near = outs[i][2:4]
        if i in vias:
            via = after(vias[i], *tokens)
            onward[i] = (to_near.astype(F32) + via.astype(F32)).astype(BF16)
            sent[i] = (own, in_row(onward[i], TERMS_ON))

    def send(i):
        own, to_near, to_far, to_back = outs[i][2:6]
        if RELAY_TERMS[i]:
            vias[i] = in_row(to_far, TERMS_OUT)
        else:
            got_far = in_row(to_far, back_of(STEP_TWO))
            sent[i] = (own, in_row(to_near, back_of(STEP_ONE)), got_far)
        group = place(Z_TERMS, i)[0]
        if i == group[-1]:
            got_z[group] = frames(to_back, -ROW)

    closed = None

    def close(i):
        nonlocal closed
        group, _, at = place(Z_TERMS, i)
        closed = tuple(close_part(firsts[i], SPLITS[i], k, sent[i] + (got_z[group],), at, k_gain, closed))

    filled, t4 = None, None
    for i in parts:
        tokens = [near[i + 1]] if i + 1 in near else []
        if i >= 2:
            relay(i - 2, outs[i - 1][7])
        if i - 2 in onward:
            tokens.append(onward[i - 2])
        for j in CLOSE_BEFORE.get(i, ()):
            close(j)
            tokens.append(closed[0])
        z_group, _, z_at = place(Z_KEYS, i)
        group, t4_heads, t4_at = place(Z_TERMS, i)
        outs[i] = attn_part(
            firsts[i], SPLITS[i], after(win, *tokens), q, k, v, g, (near[i], far[i], back[z_group]), z_at,
            q_gain, k_gain, filled, t4_heads, t4_at, t4 if t4_at else None, outs[i - 1][6:8] if i else None,
        )
        filled, t4 = tuple(outs[i][:2]), outs[i][5]
        send(i)
    relay(last - 1, *([outs[last][7]] if last > 0 else []))
    relay(last)
    gains = jnp.stack([jnp.sum(outs[last][6], axis=1), jnp.sum(outs[last][7], axis=0)])
    for i in CLOSE_AFTER:
        close(i)
    waits = [()] * 8
    known = {"on": onward.get(last - 1), "z": got_z[Z_TERMS[-1]], "y": sent[last][1:], "c": closed and closed[0], "tn": sent[max(last - 2, 0)][1]}
    for stage, names in TAIL:
        waits[stage] = tuple(jax.tree.leaves([known[n] for n in names]))
    for i in CLOSE_LAST:
        close(i)
    gains = total_over_mesh(gains, waits)
    return (filled[0][None], filled[1][None], closed[0][None], closed[1][None], gains[0], gains[1])


def solution(mesh):
    rows = P("dp", "seq", None)
    return jax.shard_map(
        on_device,
        mesh=mesh,
        in_specs=(rows, rows, rows, P(), P(), rows, rows),
        out_specs=(rows, rows, rows, rows, P(), P()),
        check_vma=False,
    )
```

```python
import functools
import math

import jax
import jax.numpy as jnp
from jax import lax
from jax.experimental import pallas as pl
from jax.experimental.pallas import tpu as pltpu
from jax.sharding import PartitionSpec as P

HEAD_DIM = 128
ROW = 4
SPLITS = (4, 4, 4)
Z_KEYS = ((0,), (1, 2))
Z_TERMS = ((0, 1), (2,))
RELAY_KEYS = (True, True, True)
RELAY_TERMS = (True, True, True)
ORDERED = True
CLOSE_BEFORE = {}
CLOSE_AFTER = (0, 1)
CLOSE_LAST = (2,)
STAGES = (("dp", 1, 2), ("dp", 2, 2), ("dp", 4, 2), ("seq", 4, 4), ("seq", 16, 2), ("seq", 1, 4))
TAIL = ((0, ("on",)), (3, ("z", "on2")), (5, ("y", "c")))
ATTN_COST = 4_000_000_000
CLOSE_COST = 1_000_000_000
F32 = jnp.float32
BF16 = jnp.bfloat16
MIB = 2**20

KEYS_OUT = ((0, 1), (1, 0), (2, 3))
KEYS_ON = ((1, 2), (0, 3))
TERMS_OUT = ((3, 0), (2, 1))
TERMS_ON = ((0, 1), (1, 0), (3, 2))
STEP_ONE = ((0, 1), (2, 3))
STEP_TWO = ((0, 2), (1, 3))


def dot(a, b):
    return lax.dot_general(a, b, (((1,), (0,)), ((), ())), preferred_element_type=F32)


def unit_rows(block):
    flat = block.astype(F32)
    root = lax.rsqrt(jnp.mean(flat * flat, axis=1, keepdims=True) + 1e-6)
    return flat * root, root


def attn_kernel(per_step, begun, win, q_ref, k_ref, v_ref, g_ref, kv1, kv2, kv4, qg_ref, kg_ref, *refs):
    (out_ref, gq_ref, own_ref, t1_ref, t2_ref, t4_ref, qsum_ref, ksum_ref) = refs[-8:]
    scale = HEAD_DIM ** (-0.5)
    to_two = scale * math.log2(math.e)

    @pl.when(pl.program_id(0) == 0)
    def _():
        qsum_ref[...] = refs[0][...] if begun else jnp.zeros_like(qsum_ref)
        ksum_ref[...] = refs[1][...] if begun else jnp.zeros_like(ksum_ref)

    q_gain = qg_ref[...]
    k_gain = kg_ref[...]
    held = [True] + [win[j] >= 0 for j in range(3)]
    terms = (own_ref, t1_ref, t2_ref, t4_ref)
    for at in range(per_step):
        cols = slice(at * HEAD_DIM, (at + 1) * HEAD_DIM)
        qt = q_ref[:, cols].T.astype(F32)
        q_root = lax.rsqrt(jnp.mean(qt * qt, axis=0, keepdims=True) + 1e-6)
        q_unit = qt * q_root
        qt_b = (q_unit * q_gain).astype(BF16)
        q_b = qt_b.T
        g_b = g_ref[:, cols]
        gt_b = g_b.T
        keys = [k_ref[:, cols]] + [ref[0, :, cols] for ref in (kv1, kv2, kv4)]
        vals = [v_ref[:, cols]] + [ref[1, :, cols] for ref in (kv1, kv2, kv4)]

        k_norm, scores, tops = [], [], []
        for j in range(4):
            k_norm.append((unit_rows(keys[j])[0] * k_gain).astype(BF16))
            scores.append(dot(k_norm[j], qt_b))
            top = jnp.max(scores[j], axis=0, keepdims=True)
            tops.append(top if j == 0 else jnp.where(held[j], top, -jnp.inf))
        row_max = functools.reduce(jnp.maximum, tops) * to_two
        raw, sums, dps = [], [], []
        for j in range(4):
            dps.append(dot(vals[j], gt_b))
            factor = to_two if j == 0 else jnp.where(held[j], to_two, 0.0)
            less = row_max if j == 0 else jnp.where(held[j], row_max, 1e30)
            raw.append(jnp.exp2(scores[j] * factor - less))
            sums.append(jnp.sum(raw[j], axis=0, keepdims=True))
        inverse = 1.0 / functools.reduce(jnp.add, sums)
        out = None
        for j in range(4):
            probs_low = (raw[j] * inverse).astype(BF16)
            terms[j][at, 1] = dot(probs_low, g_b).astype(BF16)
            o = dot(vals[j].T, probs_low)
            out = o if j == 0 else out + o
        out_low = out.astype(BF16)
        out_ref[:, cols] = out_low.T
        row_dot = jnp.sum(gt_b.astype(F32) * out_low.astype(F32), axis=0, keepdims=True)
        scaled_inverse = inverse * scale
        dq = None
        k_part = None
        for j in range(4):
            ds = (raw[j] * ((dps[j] - row_dot) * scaled_inverse)).astype(BF16)
            d = dot(k_norm[j].T, ds)
            dq = d if j == 0 else dq + d
            dk = dot(ds, q_b).astype(BF16)
            terms[j][at, 0] = dk
            part = jnp.sum((dk.astype(F32) * unit_rows(keys[j])[0]).reshape(-1, 8, HEAD_DIM), axis=0)
            k_part = part if j == 0 else k_part + part
        ksum_ref[...] += k_part
        qsum_ref[...] += dq * q_unit
        scaled = dq * q_gain
        inner = jnp.mean(scaled * q_unit, axis=0, keepdims=True)
        gq_ref[:, cols] = (q_root * (scaled - q_unit * inner)).astype(BF16).T


def attn_part(first, heads, win, q, k, v, g, pairs, z_at, q_gain, k_gain, filled, t4_shape, t4_at, t4_filled, totals):
    rows, width = q.shape
    per_step = next(n for n in (2, 1) if not any(x % n for x in (first, heads, z_at, t4_at)))
    wide = per_step * HEAD_DIM
    whole = pl.BlockSpec((rows, wide), lambda h: (0, first // per_step + h))
    smem = pl.BlockSpec(memory_space=pltpu.SMEM)
    hbm = pl.BlockSpec(memory_space=pl.ANY)

    def two_at(start):
        return pl.BlockSpec((per_step, 2, rows, HEAD_DIM), lambda h: (start // per_step + h, 0, 0, 0))

    def keys_at(start):
        return pl.BlockSpec((2, rows, wide), lambda h: (0, 0, start // per_step + h))

    def const(shape):
        return pl.BlockSpec(shape, lambda h: (0, 0))

    full = jax.ShapeDtypeStruct((rows, width), BF16)
    pair = jax.ShapeDtypeStruct((heads, 2, rows, HEAD_DIM), BF16)
    sums = [(HEAD_DIM, rows), (8, HEAD_DIM)]
    begun = totals is not None
    more = list(totals) if begun else []
    more_specs = [const(x) for x in sums] if begun else []
    kept = {6: 10, 7: 11} if begun else {}
    for out, array in ((0, filled and filled[0]), (1, filled and filled[1]), (5, t4_filled)):
        if array is not None:
            kept[out] = 10 + len(more)
            more.append(array)
            more_specs.append(hbm)
    return pl.pallas_call(
        functools.partial(attn_kernel, per_step, begun),
        grid=(heads // per_step,),
        in_specs=[smem, whole, whole, whole, whole, keys_at(0), keys_at(0), keys_at(z_at)]
        + [const((HEAD_DIM, 1)), const((1, HEAD_DIM))]
        + more_specs,
        out_specs=[whole, whole, two_at(0), two_at(0), two_at(0), two_at(t4_at)] + [const(x) for x in sums],
        out_shape=[
            full,
            full,
            pair,
            pair,
            pair,
            jax.ShapeDtypeStruct((t4_shape, 2, rows, HEAD_DIM), BF16),
            *[jax.ShapeDtypeStruct(x, F32) for x in sums],
        ],
        input_output_aliases={where: out for out, where in kept.items()},
        compiler_params=pltpu.CompilerParams(
            dimension_semantics=("arbitrary",), vmem_limit_bytes=58 * MIB
        ),
        cost_estimate=pl.CostEstimate(
            flops=heads * ATTN_COST,
            bytes_accessed=heads * ATTN_COST // 1000,
            transcendentals=0,
        ),
        name="attention_part",
    )(win, q, k, v, g, *pairs, q_gain.reshape(HEAD_DIM, 1), k_gain.reshape(1, HEAD_DIM), *more)


def close_kernel(count, k_ref, *refs):
    got, kg_ref, (gk_ref, gv_ref) = refs[:count], refs[count], refs[-2:]
    dk, dv = (functools.reduce(jnp.add, [r[0, i].astype(F32) for r in got]) for i in range(2))
    gv_ref[...] = dv.astype(BF16)
    unit, root = unit_rows(k_ref[...])
    scaled = dk * kg_ref[...]
    inner = jnp.mean(scaled * unit, axis=1, keepdims=True)
    gk_ref[...] = (root * (scaled - unit * inner)).astype(BF16)


def close_part(first, heads, k, got, z_at, k_gain, filled):
    rows, width = k.shape
    whole = pl.BlockSpec((rows, HEAD_DIM), lambda h: (0, first + h))
    two = pl.BlockSpec((1, 2, rows, HEAD_DIM), lambda h: (h, 0, 0, 0))
    two_z = pl.BlockSpec((1, 2, rows, HEAD_DIM), lambda h: (z_at + h, 0, 0, 0))
    hbm = pl.BlockSpec(memory_space=pl.ANY)
    full = jax.ShapeDtypeStruct((rows, width), BF16)
    filled = () if filled is None else filled
    count = len(got)
    return pl.pallas_call(
        functools.partial(close_kernel, count),
        grid=(heads,),
        in_specs=[whole] + [two] * (count - 1) + [two_z] + [pl.BlockSpec((1, HEAD_DIM), lambda h: (0, 0))] + [hbm] * len(filled),
        out_specs=[whole, whole],
        out_shape=[full, full],
        input_output_aliases={2 + count + i: i for i in range(len(filled))},
        compiler_params=pltpu.CompilerParams(dimension_semantics=("arbitrary",), vmem_limit_bytes=58 * MIB),
        cost_estimate=pl.CostEstimate(
            flops=heads * CLOSE_COST,
            bytes_accessed=heads * CLOSE_COST // 1000,
            transcendentals=0,
        ),
        name="close_part",
    )(k, *got, k_gain.reshape(1, HEAD_DIM), *filled)


def total_over_mesh(block, waits):
    def spread(x, axis, size, stride, group):
        def peer(i, d):
            at = i // stride % group
            return i + ((at ^ d) - at) * stride

        got = [x] + [lax.ppermute(x, axis, [(i, peer(i, d)) for i in range(size)]) for d in range(1, group)]
        while len(got) > 1:
            got = [a + b for a, b in zip(got[::2], got[1::2])]
        return got[0]

    for (axis, stride, group), others in zip(STAGES, waits):
        block = spread(after(block, *others), axis, lax.axis_size(axis), stride, group)
    return block


def after(block, *others):
    return lax.optimization_barrier((block,) + others)[0] if ORDERED and others else block


def on_device(q_in, k_in, v_in, q_gain, k_gain, window, grad_out):
    q, k, v, g = q_in[0], k_in[0], v_in[0], grad_out[0]
    rows = q.shape[0]
    win = window[0, 0]
    tiles = lax.axis_size("seq")
    starts = range(0, tiles, ROW)

    def in_row(block, hops):
        return lax.ppermute(block, "seq", [(s + a, s + b) for s in starts for a, b in hops])

    def frames(block, step):
        return lax.ppermute(
            block, "seq", [(t, t + step) for t in range(tiles) if 0 <= t + step < tiles]
        )

    def back_of(hops):
        return tuple((b, a) for a, b in hops)

    firsts = [sum(SPLITS[:i]) for i in range(len(SPLITS))]
    parts = range(len(SPLITS))
    last = len(SPLITS) - 1
    near, far, back, outs, onward, sent, got_z = {}, {}, {}, {}, {}, {}, {}

    def place(groups, i):
        group = next(g for g in groups if i in g)
        sizes = [SPLITS[j] for j in group]
        return group, sum(sizes), sum(sizes[: group.index(i)])

    def pack(first, heads):
        cols = slice(first * HEAD_DIM, (first + heads) * HEAD_DIM)
        return jnp.stack([x[:, cols] for x in (k, v)])

    for i in parts:
        mine = pack(firsts[i], SPLITS[i])
        along = mine if i == 0 else after(mine, near[i - 1])
        group, heads, _ = place(Z_KEYS, i)
        if i == group[0]:
            ours = mine if heads == SPLITS[i] else pack(firsts[i], heads)
            if i > 0:
                ours = after(ours, *list(back.values())[-1:], near[max(group[0] - 1, 0)])
            back[group] = frames(ours, ROW)
        if RELAY_KEYS[i]:
            near[i] = in_row(along, KEYS_OUT)
            far[i] = in_row(near[i], KEYS_ON)
        else:
            near[i] = in_row(along, STEP_ONE)
            far[i] = in_row(along, STEP_TWO)

    vias = {}

    def relay(i, *tokens):
        own, to_near = outs[i][2:4]
        if i in vias:
            via = after(vias[i], *tokens)
            onward[i] = (to_near.astype(F32) + via.astype(F32)).astype(BF16)
            sent[i] = (own, in_row(onward[i], TERMS_ON))

    def send(i):
        own, to_near, to_far, to_back = outs[i][2:6]
        if RELAY_TERMS[i]:
            vias[i] = in_row(to_far, TERMS_OUT)
        else:
            got_far = in_row(to_far, back_of(STEP_TWO))
            sent[i] = (own, in_row(to_near, back_of(STEP_ONE)), got_far)
        group = place(Z_TERMS, i)[0]
        if i == group[-1]:
            got_z[group] = frames(to_back, -ROW)

    closed = None

    def close(i):
        nonlocal closed
        group, _, at = place(Z_TERMS, i)
        closed = tuple(close_part(firsts[i], SPLITS[i], k, sent[i] + (got_z[group],), at, k_gain, closed))

    filled, t4 = None, None
    for i in parts:
        tokens = [near[i + 1]] if i + 1 in near else []
        if i >= 2:
            relay(i - 2, outs[i - 1][7])
        if i - 2 in onward:
            tokens.append(onward[i - 2])
        for j in CLOSE_BEFORE.get(i, ()):
            close(j)
            tokens.append(closed[0])
        z_group, _, z_at = place(Z_KEYS, i)
        group, t4_heads, t4_at = place(Z_TERMS, i)
        outs[i] = attn_part(
            firsts[i], SPLITS[i], after(win, *tokens), q, k, v, g, (near[i], far[i], back[z_group]), z_at,
            q_gain, k_gain, filled, t4_heads, t4_at, t4 if t4_at else None, outs[i - 1][6:8] if i else None,
        )
        filled, t4 = tuple(outs[i][:2]), outs[i][5]
        send(i)
    relay(last - 1, *([outs[last][7]] if last > 0 else []))
    relay(last)
    gains = jnp.stack([jnp.sum(outs[last][6], axis=1), jnp.sum(outs[last][7], axis=0)])
    for i in CLOSE_AFTER:
        close(i)
    waits = [()] * 8
    known = {"on": onward.get(last - 1), "on2": onward.get(last), "z": got_z[Z_TERMS[-1]], "y": sent[last][1:], "c": closed and closed[0], "tn": sent[max(last - 2, 0)][1]}
    for stage, names in TAIL:
        waits[stage] = tuple(jax.tree.leaves([known[n] for n in names]))
    for i in CLOSE_LAST:
        close(i)
    gains = total_over_mesh(gains, waits)
    return (filled[0][None], filled[1][None], closed[0][None], closed[1][None], gains[0], gains[1])


def solution(mesh):
    rows = P("dp", "seq", None)
    return jax.shard_map(
        on_device,
        mesh=mesh,
        in_specs=(rows, rows, rows, P(), P(), rows, rows),
        out_specs=(rows, rows, rows, rows, P(), P()),
        check_vma=False,
    )
```

```python
import functools
import math

import jax
import jax.numpy as jnp
from jax import lax
from jax.experimental import pallas as pl
from jax.experimental.pallas import tpu as pltpu
from jax.sharding import PartitionSpec as P

HEAD_DIM = 128
ROW = 4
SPLITS = (4, 4, 4)
Z_KEYS = ((0,), (1, 2))
Z_TERMS = ((0, 1), (2,))
RELAY_KEYS = (True, True, True)
RELAY_TERMS = (True, True, True)
ORDERED = True
CLOSE_BEFORE = {}
CLOSE_AFTER = (0, 1)
CLOSE_LAST = (2,)
STAGES = (("dp", 1, 2), ("dp", 2, 2), ("dp", 4, 2), ("seq", 1, 4), ("seq", 4, 4), ("seq", 16, 2))
TAIL = ((0, ("on",)), (3, ("on2",)), (4, ("z",)), (5, ("y", "c")))
ATTN_COST = 4_000_000_000
CLOSE_COST = 1_000_000_000
F32 = jnp.float32
BF16 = jnp.bfloat16
MIB = 2**20

KEYS_OUT = ((0, 1), (1, 0), (2, 3))
KEYS_ON = ((1, 2), (0, 3))
TERMS_OUT = ((3, 0), (2, 1))
TERMS_ON = ((0, 1), (1, 0), (3, 2))
STEP_ONE = ((0, 1), (2, 3))
STEP_TWO = ((0, 2), (1, 3))


def dot(a, b):
    return lax.dot_general(a, b, (((1,), (0,)), ((), ())), preferred_element_type=F32)


def unit_rows(block):
    flat = block.astype(F32)
    root = lax.rsqrt(jnp.mean(flat * flat, axis=1, keepdims=True) + 1e-6)
    return flat * root, root


def attn_kernel(per_step, begun, win, q_ref, k_ref, v_ref, g_ref, kv1, kv2, kv4, qg_ref, kg_ref, *refs):
    (out_ref, gq_ref, own_ref, t1_ref, t2_ref, t4_ref, qsum_ref, ksum_ref) = refs[-8:]
    scale = HEAD_DIM ** (-0.5)
    to_two = scale * math.log2(math.e)

    @pl.when(pl.program_id(0) == 0)
    def _():
        qsum_ref[...] = refs[0][...] if begun else jnp.zeros_like(qsum_ref)
        ksum_ref[...] = refs[1][...] if begun else jnp.zeros_like(ksum_ref)

    q_gain = qg_ref[...]
    k_gain = kg_ref[...]
    held = [True] + [win[j] >= 0 for j in range(3)]
    terms = (own_ref, t1_ref, t2_ref, t4_ref)
    for at in range(per_step):
        cols = slice(at * HEAD_DIM, (at + 1) * HEAD_DIM)
        qt = q_ref[:, cols].T.astype(F32)
        q_root = lax.rsqrt(jnp.mean(qt * qt, axis=0, keepdims=True) + 1e-6)
        q_unit = qt * q_root
        qt_b = (q_unit * q_gain).astype(BF16)
        q_b = qt_b.T
        g_b = g_ref[:, cols]
        gt_b = g_b.T
        keys = [k_ref[:, cols]] + [ref[0, :, cols] for ref in (kv1, kv2, kv4)]
        vals = [v_ref[:, cols]] + [ref[1, :, cols] for ref in (kv1, kv2, kv4)]

        k_norm, scores, tops = [], [], []
        for j in range(4):
            k_norm.append((unit_rows(keys[j])[0] * k_gain).astype(BF16))
            scores.append(dot(k_norm[j], qt_b))
            top = jnp.max(scores[j], axis=0, keepdims=True)
            tops.append(top if j == 0 else jnp.where(held[j], top, -jnp.inf))
        row_max = functools.reduce(jnp.maximum, tops) * to_two
        raw, sums, dps = [], [], []
        for j in range(4):
            dps.append(dot(vals[j], gt_b))
            factor = to_two if j == 0 else jnp.where(held[j], to_two, 0.0)
            less = row_max if j == 0 else jnp.where(held[j], row_max, 1e30)
            raw.append(jnp.exp2(scores[j] * factor - less))
            sums.append(jnp.sum(raw[j], axis=0, keepdims=True))
        inverse = 1.0 / functools.reduce(jnp.add, sums)
        out = None
        for j in range(4):
            probs_low = (raw[j] * inverse).astype(BF16)
            terms[j][at, 1] = dot(probs_low, g_b).astype(BF16)
            o = dot(vals[j].T, probs_low)
            out = o if j == 0 else out + o
        out_low = out.astype(BF16)
        out_ref[:, cols] = out_low.T
        row_dot = jnp.sum(gt_b.astype(F32) * out_low.astype(F32), axis=0, keepdims=True)
        scaled_inverse = inverse * scale
        dq = None
        k_part = None
        for j in range(4):
            ds = (raw[j] * ((dps[j] - row_dot) * scaled_inverse)).astype(BF16)
            d = dot(k_norm[j].T, ds)
            dq = d if j == 0 else dq + d
            dk = dot(ds, q_b).astype(BF16)
            terms[j][at, 0] = dk
            part = jnp.sum((dk.astype(F32) * unit_rows(keys[j])[0]).reshape(-1, 8, HEAD_DIM), axis=0)
            k_part = part if j == 0 else k_part + part
        ksum_ref[...] += k_part
        qsum_ref[...] += dq * q_unit
        scaled = dq * q_gain
        inner = jnp.mean(scaled * q_unit, axis=0, keepdims=True)
        gq_ref[:, cols] = (q_root * (scaled - q_unit * inner)).astype(BF16).T


def attn_part(first, heads, win, q, k, v, g, pairs, z_at, q_gain, k_gain, filled, t4_shape, t4_at, t4_filled, totals):
    rows, width = q.shape
    per_step = next(n for n in (2, 1) if not any(x % n for x in (first, heads, z_at, t4_at)))
    wide = per_step * HEAD_DIM
    whole = pl.BlockSpec((rows, wide), lambda h: (0, first // per_step + h))
    smem = pl.BlockSpec(memory_space=pltpu.SMEM)
    hbm = pl.BlockSpec(memory_space=pl.ANY)

    def two_at(start):
        return pl.BlockSpec((per_step, 2, rows, HEAD_DIM), lambda h: (start // per_step + h, 0, 0, 0))

    def keys_at(start):
        return pl.BlockSpec((2, rows, wide), lambda h: (0, 0, start // per_step + h))

    def const(shape):
        return pl.BlockSpec(shape, lambda h: (0, 0))

    full = jax.ShapeDtypeStruct((rows, width), BF16)
    pair = jax.ShapeDtypeStruct((heads, 2, rows, HEAD_DIM), BF16)
    sums = [(HEAD_DIM, rows), (8, HEAD_DIM)]
    begun = totals is not None
    more = list(totals) if begun else []
    more_specs = [const(x) for x in sums] if begun else []
    kept = {6: 10, 7: 11} if begun else {}
    for out, array in ((0, filled and filled[0]), (1, filled and filled[1]), (5, t4_filled)):
        if array is not None:
            kept[out] = 10 + len(more)
            more.append(array)
            more_specs.append(hbm)
    return pl.pallas_call(
        functools.partial(attn_kernel, per_step, begun),
        grid=(heads // per_step,),
        in_specs=[smem, whole, whole, whole, whole, keys_at(0), keys_at(0), keys_at(z_at)]
        + [const((HEAD_DIM, 1)), const((1, HEAD_DIM))]
        + more_specs,
        out_specs=[whole, whole, two_at(0), two_at(0), two_at(0), two_at(t4_at)] + [const(x) for x in sums],
        out_shape=[
            full,
            full,
            pair,
            pair,
            pair,
            jax.ShapeDtypeStruct((t4_shape, 2, rows, HEAD_DIM), BF16),
            *[jax.ShapeDtypeStruct(x, F32) for x in sums],
        ],
        input_output_aliases={where: out for out, where in kept.items()},
        compiler_params=pltpu.CompilerParams(
            dimension_semantics=("arbitrary",), vmem_limit_bytes=58 * MIB
        ),
        cost_estimate=pl.CostEstimate(
            flops=heads * ATTN_COST,
            bytes_accessed=heads * ATTN_COST // 1000,
            transcendentals=0,
        ),
        name="attention_part",
    )(win, q, k, v, g, *pairs, q_gain.reshape(HEAD_DIM, 1), k_gain.reshape(1, HEAD_DIM), *more)


def close_kernel(count, k_ref, *refs):
    got, kg_ref, (gk_ref, gv_ref) = refs[:count], refs[count], refs[-2:]
    dk, dv = (functools.reduce(jnp.add, [r[0, i].astype(F32) for r in got]) for i in range(2))
    gv_ref[...] = dv.astype(BF16)
    unit, root = unit_rows(k_ref[...])
    scaled = dk * kg_ref[...]
    inner = jnp.mean(scaled * unit, axis=1, keepdims=True)
    gk_ref[...] = (root * (scaled - unit * inner)).astype(BF16)


def close_part(first, heads, k, got, z_at, k_gain, filled):
    rows, width = k.shape
    whole = pl.BlockSpec((rows, HEAD_DIM), lambda h: (0, first + h))
    two = pl.BlockSpec((1, 2, rows, HEAD_DIM), lambda h: (h, 0, 0, 0))
    two_z = pl.BlockSpec((1, 2, rows, HEAD_DIM), lambda h: (z_at + h, 0, 0, 0))
    hbm = pl.BlockSpec(memory_space=pl.ANY)
    full = jax.ShapeDtypeStruct((rows, width), BF16)
    filled = () if filled is None else filled
    count = len(got)
    return pl.pallas_call(
        functools.partial(close_kernel, count),
        grid=(heads,),
        in_specs=[whole] + [two] * (count - 1) + [two_z] + [pl.BlockSpec((1, HEAD_DIM), lambda h: (0, 0))] + [hbm] * len(filled),
        out_specs=[whole, whole],
        out_shape=[full, full],
        input_output_aliases={2 + count + i: i for i in range(len(filled))},
        compiler_params=pltpu.CompilerParams(dimension_semantics=("arbitrary",), vmem_limit_bytes=58 * MIB),
        cost_estimate=pl.CostEstimate(
            flops=heads * CLOSE_COST,
            bytes_accessed=heads * CLOSE_COST // 1000,
            transcendentals=0,
        ),
        name="close_part",
    )(k, *got, k_gain.reshape(1, HEAD_DIM), *filled)


def total_over_mesh(block, waits):
    def spread(x, axis, size, stride, group):
        def peer(i, d):
            at = i // stride % group
            return i + ((at ^ d) - at) * stride

        got = [x] + [lax.ppermute(x, axis, [(i, peer(i, d)) for i in range(size)]) for d in range(1, group)]
        while len(got) > 1:
            got = [a + b for a, b in zip(got[::2], got[1::2])]
        return got[0]

    for (axis, stride, group), others in zip(STAGES, waits):
        block = spread(after(block, *others), axis, lax.axis_size(axis), stride, group)
    return block


def after(block, *others):
    return lax.optimization_barrier((block,) + others)[0] if ORDERED and others else block


def on_device(q_in, k_in, v_in, q_gain, k_gain, window, grad_out):
    q, k, v, g = q_in[0], k_in[0], v_in[0], grad_out[0]
    rows = q.shape[0]
    win = window[0, 0]
    tiles = lax.axis_size("seq")
    starts = range(0, tiles, ROW)

    def in_row(block, hops):
        return lax.ppermute(block, "seq", [(s + a, s + b) for s in starts for a, b in hops])

    def frames(block, step):
        return lax.ppermute(
            block, "seq", [(t, t + step) for t in range(tiles) if 0 <= t + step < tiles]
        )

    def back_of(hops):
        return tuple((b, a) for a, b in hops)

    firsts = [sum(SPLITS[:i]) for i in range(len(SPLITS))]
    parts = range(len(SPLITS))
    last = len(SPLITS) - 1
    near, far, back, outs, onward, sent, got_z = {}, {}, {}, {}, {}, {}, {}

    def place(groups, i):
        group = next(g for g in groups if i in g)
        sizes = [SPLITS[j] for j in group]
        return group, sum(sizes), sum(sizes[: group.index(i)])

    def pack(first, heads):
        cols = slice(first * HEAD_DIM, (first + heads) * HEAD_DIM)
        return jnp.stack([x[:, cols] for x in (k, v)])

    for i in parts:
        mine = pack(firsts[i], SPLITS[i])
        along = mine if i == 0 else after(mine, near[i - 1])
        group, heads, _ = place(Z_KEYS, i)
        if i == group[0]:
            ours = mine if heads == SPLITS[i] else pack(firsts[i], heads)
            if i > 0:
                ours = after(ours, *list(back.values())[-1:], near[max(group[0] - 1, 0)])
            back[group] = frames(ours, ROW)
        if RELAY_KEYS[i]:
            near[i] = in_row(along, KEYS_OUT)
            far[i] = in_row(near[i], KEYS_ON)
        else:
            near[i] = in_row(along, STEP_ONE)
            far[i] = in_row(along, STEP_TWO)

    vias = {}

    def relay(i, *tokens):
        own, to_near = outs[i][2:4]
        if i in vias:
            via = after(vias[i], *tokens)
            onward[i] = (to_near.astype(F32) + via.astype(F32)).astype(BF16)
            sent[i] = (own, in_row(onward[i], TERMS_ON))

    def send(i):
        own, to_near, to_far, to_back = outs[i][2:6]
        if RELAY_TERMS[i]:
            vias[i] = in_row(to_far, TERMS_OUT)
        else:
            got_far = in_row(to_far, back_of(STEP_TWO))
            sent[i] = (own, in_row(to_near, back_of(STEP_ONE)), got_far)
        group = place(Z_TERMS, i)[0]
        if i == group[-1]:
            got_z[group] = frames(to_back, -ROW)

    closed = None

    def close(i):
        nonlocal closed
        group, _, at = place(Z_TERMS, i)
        closed = tuple(close_part(firsts[i], SPLITS[i], k, sent[i] + (got_z[group],), at, k_gain, closed))

    filled, t4 = None, None
    for i in parts:
        tokens = [near[i + 1]] if i + 1 in near else []
        if i >= 2:
            relay(i - 2, outs[i - 1][7])
        if i - 2 in onward:
            tokens.append(onward[i - 2])
        for j in CLOSE_BEFORE.get(i, ()):
            close(j)
            tokens.append(closed[0])
        z_group, _, z_at = place(Z_KEYS, i)
        group, t4_heads, t4_at = place(Z_TERMS, i)
        outs[i] = attn_part(
            firsts[i], SPLITS[i], after(win, *tokens), q, k, v, g, (near[i], far[i], back[z_group]), z_at,
            q_gain, k_gain, filled, t4_heads, t4_at, t4 if t4_at else None, outs[i - 1][6:8] if i else None,
        )
        filled, t4 = tuple(outs[i][:2]), outs[i][5]
        send(i)
    relay(last - 1, *([outs[last][7]] if last > 0 else []))
    relay(last)
    gains = jnp.stack([jnp.sum(outs[last][6], axis=1), jnp.sum(outs[last][7], axis=0)])
    for i in CLOSE_AFTER:
        close(i)
    waits = [()] * 8
    known = {"on": onward.get(last - 1), "on2": onward.get(last), "z": got_z[Z_TERMS[-1]], "y": sent[last][1:], "c": closed and closed[0], "tn": sent[max(last - 2, 0)][1]}
    for stage, names in TAIL:
        waits[stage] = tuple(jax.tree.leaves([known[n] for n in names]))
    for i in CLOSE_LAST:
        close(i)
    gains = total_over_mesh(gains, waits)
    return (filled[0][None], filled[1][None], closed[0][None], closed[1][None], gains[0], gains[1])


def solution(mesh):
    rows = P("dp", "seq", None)
    return jax.shard_map(
        on_device,
        mesh=mesh,
        in_specs=(rows, rows, rows, P(), P(), rows, rows),
        out_specs=(rows, rows, rows, rows, P(), P()),
        check_vma=False,
    )
```
